32 devices in a mesh: dp: 4 (over y, core), tensor: 8 (over z, x).
Axes of the slice: x: 2, y: 2, z: 4, core: 2. Of those that a mesh axis runs over, the one named last changes fastest.
Arguments:
- loader_rows: bfloat16 [4, 8, 128, 4096], P('dp', 'tensor'), may hold values from -23 to 23
- row_counts: int32 [4, 8], P('dp', 'tensor'), may hold values from 0 to 128
- row_targets: int32 [4, 8, 128], P('dp', 'tensor'), may hold values from 0 to 255, as said below
- gate_weight: bfloat16 [4096, 16384], P('dp', 'tensor'), may hold values from -0.09375 to 0.09375
- up_weight: bfloat16 [4096, 16384], P('dp', 'tensor'), may hold values from -0.09375 to 0.09375
- down_weight: bfloat16 [16384, 4096], P('tensor'), may hold values from -0.046875 to 0.046875
Outputs:
- layer_out: bfloat16 [2048, 4096], P(('dp', 'tensor'))
The draws below stay inside these ranges and needn't reach their ends.
Inputs may be any that keep to these rules, and one draw needn't show every extreme that they name: `row_targets`: among the first row_counts[d, t] slots of replica d and tensor index t, a value v names row v % 64 of the rows of tensor index t on replica v // 64; over all replicas each such row is named exactly once, and no device names more than 32 rows of one replica. Slots past the count hold arbitrary values of the same range.
All inputs are finite; a program needn't handle non-finite values.
Results may differ from the reference program's by a relative error of at most 0.0095.
Values may be sent and summed in bfloat16 or wider, within the bound.
A program may use at most 128 MiB of HBM per device.

```python
import math
import jax
import jax.numpy as jnp
from jax import lax

D = 4096
FF = 16384
ROWS_GRP = 512
ROWS_TP = 64
CAP = 32
SLOTS = 128
TOKENS = 2048
N_DP = 4
N_TENSOR = 8


def draw_plan(key):
    item_count = N_DP * CAP
    key_favored, key_bias, key_jitter, key_shuffle, key_filler = jax.random.split(jax.random.fold_in(key, 7), 5)
    key_common = jax.random.fold_in(key, 13)
    favored = jax.random.randint(key_favored, (N_TENSOR, N_DP), 0, N_DP).astype(jnp.int32)
    common_index = jax.random.randint(key_common, (), 0, N_TENSOR).astype(jnp.int32)
    common_row = jnp.arange(N_TENSOR, dtype=jnp.int32)[:, None] == common_index
    favored = jnp.where(common_row, jnp.broadcast_to(favored[:, :1], (N_TENSOR, N_DP)), favored).astype(jnp.int32)
    heavy_bias = jax.random.randint(key_bias, (N_TENSOR, 1, N_DP), 0, 2 ** 14).astype(jnp.int32)
    jitter = jax.random.randint(key_jitter, (N_TENSOR, N_DP, item_count), 0, 2 ** 14).astype(jnp.int32)
    item_index = jnp.arange(item_count, dtype=jnp.int32)
    source = item_index // CAP
    item_score = (jitter + jnp.repeat(heavy_bias, CAP, axis=2)) * item_count + item_index[None, None, :]
    item_score = jnp.where(source[None, None, :] == favored[:, :, None], item_index[None, None, :] - item_count, item_score)
    item_order = jnp.argsort(item_score, axis=2)
    slot_rank = jnp.argsort(item_order, axis=2).astype(jnp.int32)
    chosen = slot_rank < ROWS_TP
    is_live = chosen.reshape(N_TENSOR, N_DP, N_DP, CAP).transpose(0, 2, 1, 3).reshape(N_TENSOR, N_DP, item_count)
    target_row = jnp.arange(N_DP, dtype=jnp.int32)[None, :, None, None] * ROWS_TP + slot_rank.reshape(N_TENSOR, N_DP, N_DP, CAP)
    target_row = target_row.transpose(0, 2, 1, 3).reshape(N_TENSOR, N_DP, item_count)
    shuffle_key = jax.random.randint(key_shuffle, (N_TENSOR, N_DP, item_count), 0, 2 ** 14).astype(jnp.int32) * item_count + item_index[None, None, :]
    shuffle_key = jnp.where(is_live, shuffle_key, shuffle_key + 2 ** 24)
    shuffle_order = jnp.argsort(shuffle_key, axis=2)
    live_sorted = jnp.take_along_axis(is_live, shuffle_order, axis=2)
    target_sorted = jnp.take_along_axis(target_row, shuffle_order, axis=2)
    filler = jax.random.randint(key_filler, (N_TENSOR, N_DP, item_count), 0, N_DP * ROWS_TP).astype(jnp.int32)
    targets = jnp.where(live_sorted, target_sorted, filler).astype(jnp.int32)
    counts = jnp.sum(is_live.astype(jnp.int32), axis=2).astype(jnp.int32)
    return (counts.transpose(1, 0), targets.transpose(1, 0, 2))


def draw_row_counts(key, part):
    return draw_plan(key)[0]


def draw_row_targets(key, part):
    return draw_plan(key)[1]


def draw_loader_rows(key, part):
    key_base, key_rows, key_cols = jax.random.split(jax.random.fold_in(key, 11), 3)
    shape = (N_DP, N_TENSOR, SLOTS, D)
    base_draw = jnp.clip(jax.random.normal(key_base, shape, jnp.float32), -5.0, 5.0)
    row_scale = jnp.exp(jax.random.uniform(key_rows, (N_DP, N_TENSOR, SLOTS, 1), jnp.float32, math.log(0.3), math.log(3.0)))
    col_scale = jax.random.uniform(key_cols, (D,), jnp.float32, 0.5, 1.5)
    return (base_draw * row_scale * col_scale).astype(jnp.bfloat16)


def block_scale(stream_key, dims, pieces, least, largest):
    gain = 1.0
    for position, shards_of in pieces:
        steps = jax.random.uniform(jax.random.fold_in(jax.random.fold_in(stream_key, 6), position), (shards_of,), jnp.float32, least / len(pieces), largest / len(pieces))
        gain = gain * jnp.repeat(jnp.exp(steps), dims[position] // shards_of).reshape((-1,) + (1,) * (len(dims) - 1 - position))
    return gain


def normal_values(rng, shape, spread, limit, shards=(), kind=jnp.bfloat16):
    level = block_scale(rng, shape, shards, -0.22, 0.18) if shards else 1.0
    array = jax.random.normal(rng, shape, jnp.float32) * spread * level
    return jnp.minimum(jnp.maximum(array, -limit), limit).astype(kind)


def setup_inputs(seed: int = 0) -> dict:
    arg_keys = jax.random.split(jax.random.key(seed), 7)
    loader_rows = draw_loader_rows(jax.random.fold_in(arg_keys[6], 71), 0)
    row_counts = draw_row_counts(jax.random.fold_in(arg_keys[6], 71), 0)
    row_targets = draw_row_targets(jax.random.fold_in(arg_keys[6], 71), 0)
    gate_weight = normal_values(arg_keys[3], (D, FF), D ** -0.5, 0.09375, ((0, 4), (1, 8)))
    up_weight = normal_values(arg_keys[4], (D, FF), D ** -0.5, 0.09375, ((0, 4), (1, 8)))
    down_weight = normal_values(arg_keys[5], (FF, D), FF ** -0.5, 0.046875, ((0, 8),))
    return dict(loader_rows=loader_rows, row_counts=row_counts, row_targets=row_targets, gate_weight=gate_weight, up_weight=up_weight, down_weight=down_weight)


def reference(loader_rows, row_counts, row_targets, gate_weight, up_weight, down_weight):
    shard_rows = ROWS_GRP // N_TENSOR
    slot_index = jnp.arange(SLOTS, dtype=jnp.int32)
    is_live = slot_index[None, None, :] < row_counts[:, :, None]
    tensor_index = jnp.arange(N_TENSOR, dtype=jnp.int32)[None, :, None]
    where_to = row_targets // shard_rows * ROWS_GRP + tensor_index * shard_rows + row_targets % shard_rows
    live_values = jnp.where(is_live[..., None], loader_rows.astype(jnp.float32), jnp.float32(0.0))
    batch = jnp.zeros((TOKENS, D), jnp.float32).at[where_to.reshape(-1).astype(jnp.int32)].add(live_values.reshape(-1, D))
    batch = batch.astype(jnp.bfloat16)
    wide_batch = batch.astype(jnp.float32)
    normed = (wide_batch * lax.rsqrt(lax.optimization_barrier(jnp.mean(wide_batch * wide_batch, axis=1, keepdims=True)) + 1e-05)).astype(jnp.bfloat16)
    gate_act = jnp.dot(normed, gate_weight, preferred_element_type=jnp.float32)
    up_act = jnp.dot(normed, up_weight, preferred_element_type=jnp.float32)
    hidden = (jax.nn.silu(gate_act) * up_act).astype(jnp.bfloat16)
    block_width = FF // N_TENSOR
    hidden_blocks = hidden.reshape(TOKENS, N_TENSOR, block_width).transpose(1, 0, 2)
    down_blocks = down_weight.reshape(N_TENSOR, block_width, D)

    def add_block(total_sum, block_pair):
        block_term = jnp.dot(block_pair[0], block_pair[1], preferred_element_type=jnp.float32)
        block_term = lax.optimization_barrier(block_term.astype(jnp.bfloat16)).astype(jnp.float32)
        return (total_sum + block_term, None)
    total_sum, unused = lax.scan(add_block, jnp.zeros((TOKENS, D), jnp.float32), (hidden_blocks, down_blocks))
    return (wide_batch + total_sum).astype(jnp.bfloat16)
```

```python
import jax
import jax.numpy as jnp
from jax import lax
from jax.sharding import PartitionSpec as P

ROWS_GRP = 512


def swiglu(inputs, gate_full, up_full):
    gate_act = jnp.dot(inputs, gate_full, preferred_element_type=jnp.float32)
    up_act = jnp.dot(inputs, up_full, preferred_element_type=jnp.float32)
    return (jax.nn.silu(gate_act) * up_act).astype(jnp.bfloat16)


def normalize(row_block):
    wide_rows = row_block.astype(jnp.float32)
    return (
        wide_rows * lax.rsqrt(jnp.mean(wide_rows * wide_rows, axis=1, keepdims=True) + 1e-05)
    ).astype(jnp.bfloat16)


def rounded_term(hidden_part, weights):
    partial_sum = jnp.dot(hidden_part, weights, preferred_element_type=jnp.float32)
    return lax.optimization_barrier(partial_sum.astype(jnp.bfloat16)).astype(jnp.float32)


def rebalance(loader_rows, row_counts, row_targets):
    dp_count = lax.axis_size("dp")
    tp_count = lax.axis_size("tensor")
    slot_rows = loader_rows[0, 0]
    slot_targets = row_targets[0, 0]
    live_count = row_counts[0, 0]
    slot_count = slot_rows.shape[0]
    feature_count = slot_rows.shape[1]
    per_peer = slot_count // dp_count
    shard_rows = ROWS_GRP // tp_count
    slot_index = jnp.arange(slot_count, dtype=jnp.int32)
    is_live = slot_index < live_count
    peer_index = slot_targets // shard_rows
    row_place = slot_targets % shard_rows
    peer_hot = (
        (peer_index[:, None] == jnp.arange(dp_count, dtype=jnp.int32)[None, :]) & is_live[:, None]
    ).astype(jnp.int32)
    earlier = jnp.cumsum(peer_hot, axis=0) - peer_hot
    slot_rank = jnp.sum(earlier * peer_hot, axis=1)
    send_slot = peer_index * per_peer + slot_rank
    pick_matrix = (send_slot[None, :] == slot_index[:, None]) & is_live[None, :]
    outgoing = jnp.dot(
        pick_matrix.astype(jnp.bfloat16), slot_rows, preferred_element_type=jnp.float32
    ).astype(jnp.bfloat16)
    out_place = jnp.sum(jnp.where(pick_matrix, row_place[None, :] + 1, 0), axis=1) - 1
    arrived, arrived_place = (
        lax.all_to_all(
            outgoing.reshape(dp_count, per_peer, feature_count),
            "dp",
            split_axis=0,
            concat_axis=0,
            tiled=True,
        ),
        lax.all_to_all(
            out_place.reshape(dp_count, per_peer), "dp", split_axis=0, concat_axis=0, tiled=True
        ),
    )
    land_matrix = (
        arrived_place.reshape(slot_count)[None, :]
        == jnp.arange(shard_rows, dtype=jnp.int32)[:, None]
    ).astype(jnp.bfloat16)
    local_batch = jnp.dot(
        land_matrix, arrived.reshape(slot_count, feature_count), preferred_element_type=jnp.float32
    ).astype(jnp.bfloat16)
    return local_batch


def gathered_plan(loader_rows, row_counts, row_targets, gate_weight, up_weight, down_weight):
    local_batch = rebalance(loader_rows, row_counts, row_targets)
    gate_full, up_full = (
        lax.all_gather(gate_weight, "dp", axis=0, tiled=True),
        lax.all_gather(up_weight, "dp", axis=0, tiled=True),
    )
    travelling = normalize(local_batch)
    hidden = swiglu(lax.all_gather(travelling, "tensor", axis=0, tiled=True), gate_full, up_full)
    summed = lax.psum_scatter(
        rounded_term(hidden, down_weight).astype(jnp.bfloat16),
        "tensor",
        scatter_dimension=0,
        tiled=True,
    ).astype(jnp.float32)
    return (local_batch.astype(jnp.float32) + summed).astype(jnp.bfloat16)


def swap(value, axis, mask):
    size = lax.axis_size(axis)
    return lax.ppermute(value, axis, [(i, i ^ mask) for i in range(size)])


def column_block(rows, index, width):
    return lax.dynamic_slice_in_dim(rows, index * width, width, axis=1)


def chip_plan(loader_rows, row_counts, row_targets, gate_weight, up_weight, down_weight):
    me = lax.axis_index("dp")
    width = gate_weight.shape[0]
    z_count = lax.axis_size("tensor") // 2
    gate_half = jnp.concatenate([gate_weight, swap(gate_weight, "dp", 1)], axis=0)
    up_half = jnp.concatenate([up_weight, swap(up_weight, "dp", 1)], axis=0)
    local_batch = rebalance(loader_rows, row_counts, row_targets)
    shard_rows = local_batch.shape[0]
    travelling = normalize(local_batch)
    mine = jnp.concatenate(
        [column_block(travelling, me, width), column_block(travelling, me ^ 1, width)], axis=1
    )
    theirs = jnp.concatenate(
        [column_block(travelling, me ^ 2, width), column_block(travelling, me ^ 3, width)], axis=1
    )
    block = jnp.concatenate([swap(theirs, "dp", 2), mine], axis=0)
    blocks = [block] + [swap(block, "tensor", 2 * step) for step in range(1, z_count)]
    total = local_batch.astype(jnp.float32)
    for step in range(z_count):
        near = blocks[step]
        far = swap(near, "tensor", 1)
        rows = jnp.concatenate(
            [near[:shard_rows], far[:shard_rows], near[shard_rows:], far[shard_rows:]], axis=0
        )
        half = 2 * shard_rows
        gate_act = jnp.dot(rows, gate_half, preferred_element_type=jnp.float32)
        gate_other = swap(gate_act[:half].astype(jnp.bfloat16), "dp", 2)
        up_act = jnp.dot(rows, up_half, preferred_element_type=jnp.float32)
        up_other = swap(up_act[:half].astype(jnp.bfloat16), "dp", 2)
        gate_sum = gate_act[half:] + gate_other.astype(jnp.float32)
        up_sum = up_act[half:] + up_other.astype(jnp.float32)
        hidden = (jax.nn.silu(gate_sum) * up_sum).astype(jnp.bfloat16)
        term = jnp.dot(hidden, down_weight, preferred_element_type=jnp.float32).astype(jnp.bfloat16)
        from_x = swap(term[shard_rows:], "tensor", 1)
        pair_sum = term[:shard_rows].astype(jnp.float32) + from_x.astype(jnp.float32)
        if step:
            pair_sum = swap(pair_sum.astype(jnp.bfloat16), "tensor", 2 * step).astype(jnp.float32)
        total = total + pair_sum
    return total.astype(jnp.bfloat16)


def per_device(*args):
    if lax.axis_size("dp") == 4 and lax.axis_size("tensor") == 8:
        return chip_plan(*args)
    return gathered_plan(*args)


def solution(mesh):
    placed = (
        P("dp", "tensor", None, None),
        P("dp", "tensor"),
        P("dp", "tensor", None),
        P("dp", "tensor"),
        P("dp", "tensor"),
        P("tensor", None),
    )
    return jax.shard_map(
        per_device, mesh=mesh, in_specs=placed, out_specs=P(("dp", "tensor"), None), check_vma=False
    )
```

```python
import functools

import jax
import jax.numpy as jnp
from jax import lax
from jax.experimental import pallas as pl
from jax.experimental.pallas import tpu as pltpu
from jax.sharding import PartitionSpec as P

ROWS_GRP = 512
MESH = pl.DeviceIdType.MESH


def swiglu(inputs, gate_full, up_full):
    gate_act = jnp.dot(inputs, gate_full, preferred_element_type=jnp.float32)
    up_act = jnp.dot(inputs, up_full, preferred_element_type=jnp.float32)
    return (jax.nn.silu(gate_act) * up_act).astype(jnp.bfloat16)


def normalize(row_block):
    wide_rows = row_block.astype(jnp.float32)
    return (
        wide_rows * lax.rsqrt(jnp.mean(wide_rows * wide_rows, axis=1, keepdims=True) + 1e-05)
    ).astype(jnp.bfloat16)


def rounded_term(hidden_part, weights):
    partial_sum = jnp.dot(hidden_part, weights, preferred_element_type=jnp.float32)
    return lax.optimization_barrier(partial_sum.astype(jnp.bfloat16)).astype(jnp.float32)


def rebalance(loader_rows, row_counts, row_targets):
    dp_count = lax.axis_size("dp")
    tp_count = lax.axis_size("tensor")
    slot_rows = loader_rows[0, 0]
    slot_targets = row_targets[0, 0]
    live_count = row_counts[0, 0]
    slot_count = slot_rows.shape[0]
    feature_count = slot_rows.shape[1]
    per_peer = slot_count // dp_count
    shard_rows = ROWS_GRP // tp_count
    slot_index = jnp.arange(slot_count, dtype=jnp.int32)
    is_live = slot_index < live_count
    peer_index = slot_targets // shard_rows
    row_place = slot_targets % shard_rows
    peer_hot = (
        (peer_index[:, None] == jnp.arange(dp_count, dtype=jnp.int32)[None, :]) & is_live[:, None]
    ).astype(jnp.int32)
    earlier = jnp.cumsum(peer_hot, axis=0) - peer_hot
    slot_rank = jnp.sum(earlier * peer_hot, axis=1)
    send_slot = peer_index * per_peer + slot_rank
    pick_matrix = (send_slot[None, :] == slot_index[:, None]) & is_live[None, :]
    outgoing = jnp.dot(
        pick_matrix.astype(jnp.bfloat16), slot_rows, preferred_element_type=jnp.float32
    ).astype(jnp.bfloat16)
    out_place = jnp.sum(jnp.where(pick_matrix, row_place[None, :] + 1, 0), axis=1) - 1
    arrived, arrived_place = (
        lax.all_to_all(
            outgoing.reshape(dp_count, per_peer, feature_count),
            "dp",
            split_axis=0,
            concat_axis=0,
            tiled=True,
        ),
        lax.all_to_all(
            out_place.reshape(dp_count, per_peer), "dp", split_axis=0, concat_axis=0, tiled=True
        ),
    )
    land_matrix = (
        arrived_place.reshape(slot_count)[None, :]
        == jnp.arange(shard_rows, dtype=jnp.int32)[:, None]
    ).astype(jnp.bfloat16)
    local_batch = jnp.dot(
        land_matrix, arrived.reshape(slot_count, feature_count), preferred_element_type=jnp.float32
    ).astype(jnp.bfloat16)
    return local_batch


def gathered_plan(loader_rows, row_counts, row_targets, gate_weight, up_weight, down_weight):
    local_batch = rebalance(loader_rows, row_counts, row_targets)
    gate_full, up_full = (
        lax.all_gather(gate_weight, "dp", axis=0, tiled=True),
        lax.all_gather(up_weight, "dp", axis=0, tiled=True),
    )
    travelling = normalize(local_batch)
    hidden = swiglu(lax.all_gather(travelling, "tensor", axis=0, tiled=True), gate_full, up_full)
    summed = lax.psum_scatter(
        rounded_term(hidden, down_weight).astype(jnp.bfloat16),
        "tensor",
        scatter_dimension=0,
        tiled=True,
    ).astype(jnp.float32)
    return (local_batch.astype(jnp.float32) + summed).astype(jnp.bfloat16)


def ff_kernel(
    order, norm_ref, batch_ref, gate_ref, up_ref, down_ref, out_ref,
    gate_v, up_v, down_v, rows_v, part_out, part_in, hidden_v, term_v, x_in, z_in,
    local_sem, send_sem, recv_sem,
):
    me = lax.axis_index("dp")
    place = lax.axis_index("tensor")
    core, y = lax.rem(me, 2), lax.div(me, 2)
    x, z = lax.rem(place, 2), lax.div(place, 2)
    core_peer = {"dp": 2 * y + 1 - core}
    y_peer = {"dp": 2 * (1 - y) + core}
    x_peer = {"tensor": 2 * z + 1 - x}
    z_peer = {
        1: {"tensor": 2 * (z + 1 - 2 * lax.rem(z, 2)) + x},
        2: {"tensor": 2 * lax.rem(z + 2, 4) + x},
        3: {"tensor": 2 * (3 - z) + x},
    }
    shard_rows = norm_ref.shape[0]
    half = norm_ref.shape[1] // 2
    width = gate_ref.shape[0]
    hidden_width = gate_ref.shape[1]
    tile = 512

    barrier = pltpu.get_barrier_semaphore()
    for peer in (core_peer, y_peer, x_peer, z_peer[1], z_peer[2], z_peer[3]):
        pl.semaphore_signal(barrier, inc=1, device_id=peer, device_id_type=MESH)
    pl.semaphore_wait(barrier, 6)

    def send(index, src, dst, peer):
        copy = pltpu.make_async_remote_copy(
            src_ref=src,
            dst_ref=dst,
            send_sem=send_sem.at[index],
            recv_sem=recv_sem.at[index],
            device_id=peer,
            device_id_type=MESH,
        )
        copy.start()
        sent.append(copy)
        return copy

    sent = []
    own_cols = pl.ds(pl.multiple_of(y * half, half), half)
    peer_cols = pl.ds(pl.multiple_of((1 - y) * half, half), half)
    own_block = pl.ds(pl.multiple_of(core * width, width), width)
    first = send(
        0, norm_ref.at[:, peer_cols], rows_v.at[0, 0, pl.ds(0, shard_rows), :], y_peer
    )
    own_rows = pltpu.make_async_copy(
        norm_ref.at[:, own_cols], rows_v.at[0, 1, pl.ds(0, shard_rows), :], local_sem.at[0]
    )
    own_rows.start()
    gate_swap = send(1, gate_ref, gate_v.at[own_block, :], core_peer)
    gate_own = pltpu.make_async_copy(gate_ref, gate_v.at[own_block, :], local_sem.at[1])
    gate_own.start()
    up_swap = send(2, up_ref, up_v.at[own_block, :], core_peer)
    up_own = pltpu.make_async_copy(up_ref, up_v.at[own_block, :], local_sem.at[2])
    up_own.start()
    down_own = pltpu.make_async_copy(down_ref, down_v, local_sem.at[3])
    down_own.start()

    near = pl.ds(0, shard_rows)
    far = pl.ds(shard_rows, shard_rows)
    own_rows.wait()
    first.wait_recv()
    z_copy, x_copy = {}, {}

    def spread(step):
        z_copy[step] = send(
            2 + step, rows_v.at[0, :, near, :], rows_v.at[step, :, near, :], z_peer[step]
        )

    def cross(step):
        if step:
            z_copy[step].wait_recv()
        x_copy[step] = send(
            6 + step, rows_v.at[step, :, near, :], rows_v.at[step, :, far, :], x_peer
        )

    parts = {}

    def project(step):
        x_copy[step].wait_recv()
        for which, weight in ((0, gate_v), (1, up_v)):
            if step == order[0]:
                (gate_swap, up_swap)[which].wait_recv()
                (gate_own, up_own)[which].wait()

            def body(i, carry):
                cols = pl.ds(pl.multiple_of(i * tile, tile), tile)
                part_out[step, which, :, cols] = jnp.dot(
                    rows_v[step, 0], weight[:, cols], preferred_element_type=jnp.float32
                ).astype(jnp.bfloat16)
                return carry

            lax.fori_loop(0, hidden_width // tile, body, 0)
            parts[step, which] = send(
                10 + 2 * step + which, part_out.at[step, which], part_in.at[step, which], y_peer
            )

    term_copy, pair_copy = {}, {}

    def finish(step):
        parts[step, 0].wait_recv()
        parts[step, 1].wait_recv()

        def body(i, carry):
            cols = pl.ds(pl.multiple_of(i * tile, tile), tile)
            rows = rows_v[step, 1]
            gate_sum = jnp.dot(
                rows, gate_v[:, cols], preferred_element_type=jnp.float32
            ) + part_in[step, 0, :, cols].astype(jnp.float32)
            up_sum = jnp.dot(
                rows, up_v[:, cols], preferred_element_type=jnp.float32
            ) + part_in[step, 1, :, cols].astype(jnp.float32)
            hidden_v[:, cols] = (gate_sum / (1.0 + jnp.exp(-gate_sum)) * up_sum).astype(
                jnp.bfloat16
            )
            return carry

        lax.fori_loop(0, hidden_width // tile, body, 0)
        if step == order[0]:
            down_own.wait()

        def down_body(i, carry):
            cols = pl.ds(pl.multiple_of(i * tile, tile), tile)
            term_v[step, :, cols] = jnp.dot(
                hidden_v[...], down_v[:, cols], preferred_element_type=jnp.float32
            ).astype(jnp.bfloat16)
            return carry

        lax.fori_loop(0, 2 * half // tile, down_body, 0)
        term_copy[step] = send(18 + step, term_v.at[step, far, :], x_in.at[step], x_peer)

    def pair(step):
        term_copy[step].wait_recv()
        term_v[step, near, :] = (
            term_v[step, near, :].astype(jnp.float32) + x_in[step].astype(jnp.float32)
        ).astype(jnp.bfloat16)
        pair_copy[step] = send(21 + step, term_v.at[step, near, :], z_in.at[step - 1], z_peer[step])

    s0, s1, s2, s3 = order
    cross(s0)
    spread(s1)
    project(s0)
    spread(s2)
    cross(s1)
    project(s1)
    spread(s3)
    cross(s2)
    finish(s0)
    project(s2)
    cross(s3)
    finish(s1)
    project(s3)
    pair(s1)
    finish(s2)
    pair(s2)
    finish(s3)
    pair(s3)
    term_copy[0].wait_recv()
    total = (
        batch_ref[...].astype(jnp.float32)
        + term_v[0, near, :].astype(jnp.float32)
        + x_in[0].astype(jnp.float32)
    )
    for step in (s1, s2, s3):
        pair_copy[step].wait_recv()
        total = total + z_in[step - 1].astype(jnp.float32)
    out_ref[...] = total.astype(jnp.bfloat16)
    for copy in sent:
        copy.wait_send()


def chip_plan(loader_rows, row_counts, row_targets, gate_weight, up_weight, down_weight):
    local_batch = rebalance(loader_rows, row_counts, row_targets)
    travelling = normalize(local_batch)
    shard_rows, features = local_batch.shape
    hidden_width = gate_weight.shape[1]
    half = features // 2
    vmem = pl.BlockSpec(memory_space=pltpu.VMEM)
    any_space = pl.BlockSpec(memory_space=pl.ANY)
    bf16 = jnp.bfloat16
    return pl.pallas_call(
        functools.partial(ff_kernel, (0, 2, 3, 1)),
        out_shape=jax.ShapeDtypeStruct((shard_rows, features), bf16),
        in_specs=[vmem, vmem, any_space, any_space, any_space],
        out_specs=vmem,
        scratch_shapes=[
            pltpu.VMEM((half, hidden_width), bf16),
            pltpu.VMEM((half, hidden_width), bf16),
            pltpu.VMEM((hidden_width, features), bf16),
            pltpu.VMEM((4, 2, 2 * shard_rows, half), bf16),
            pltpu.VMEM((4, 2, 2 * shard_rows, hidden_width), bf16),
            pltpu.VMEM((4, 2, 2 * shard_rows, hidden_width), bf16),
            pltpu.VMEM((2 * shard_rows, hidden_width), bf16),
            pltpu.VMEM((4, 2 * shard_rows, features), bf16),
            pltpu.VMEM((4, shard_rows, features), bf16),
            pltpu.VMEM((3, shard_rows, features), bf16),
            pltpu.SemaphoreType.DMA((4,)),
            pltpu.SemaphoreType.DMA((25,)),
            pltpu.SemaphoreType.DMA((25,)),
        ],
        compiler_params=pltpu.CompilerParams(
            collective_id=0, has_side_effects=True, vmem_limit_bytes=60 * 1024 * 1024
        ),
        cost_estimate=pl.CostEstimate(
            flops=26 * 10**9, bytes_accessed=26 * 2**20, transcendentals=2**20
        ),
    )(travelling, local_batch, gate_weight, up_weight, down_weight)


def per_device(*args):
    if lax.axis_size("dp") == 4 and lax.axis_size("tensor") == 8:
        return chip_plan(*args)
    return gathered_plan(*args)


def solution(mesh):
    placed = (
        P("dp", "tensor", None, None),
        P("dp", "tensor"),
        P("dp", "tensor", None),
        P("dp", "tensor"),
        P("dp", "tensor"),
        P("tensor", None),
    )
    return jax.shard_map(
        per_device, mesh=mesh, in_specs=placed, out_specs=P(("dp", "tensor"), None), check_vma=False
    )
```

```python
import jax
import jax.numpy as jnp
from jax import lax
from jax.experimental import pallas as pl
from jax.experimental.pallas import tpu as pltpu
from jax.sharding import PartitionSpec as P

ROWS_GRP = 512
MESH = pl.DeviceIdType.MESH


def swiglu(inputs, gate_full, up_full):
    gate_act = jnp.dot(inputs, gate_full, preferred_element_type=jnp.float32)
    up_act = jnp.dot(inputs, up_full, preferred_element_type=jnp.float32)
    return (jax.nn.silu(gate_act) * up_act).astype(jnp.bfloat16)


def normalize(row_block):
    wide_rows = row_block.astype(jnp.float32)
    return (
        wide_rows * lax.rsqrt(jnp.mean(wide_rows * wide_rows, axis=1, keepdims=True) + 1e-05)
    ).astype(jnp.bfloat16)


def rounded_term(hidden_part, weights):
    partial_sum = jnp.dot(hidden_part, weights, preferred_element_type=jnp.float32)
    return lax.optimization_barrier(partial_sum.astype(jnp.bfloat16)).astype(jnp.float32)


def pick_slots(loader_rows, row_counts, row_targets):
    dp_count = lax.axis_size("dp")
    tp_count = lax.axis_size("tensor")
    slot_rows = loader_rows[0, 0]
    slot_targets = row_targets[0, 0]
    live_count = row_counts[0, 0]
    slot_count = slot_rows.shape[0]
    feature_count = slot_rows.shape[1]
    per_peer = slot_count // dp_count
    shard_rows = ROWS_GRP // tp_count
    slot_index = jnp.arange(slot_count, dtype=jnp.int32)
    is_live = slot_index < live_count
    peer_index = slot_targets // shard_rows
    row_place = slot_targets % shard_rows
    peer_hot = (
        (peer_index[:, None] == jnp.arange(dp_count, dtype=jnp.int32)[None, :]) & is_live[:, None]
    ).astype(jnp.int32)
    earlier = jnp.cumsum(peer_hot, axis=0) - peer_hot
    slot_rank = jnp.sum(earlier * peer_hot, axis=1)
    send_slot = peer_index * per_peer + slot_rank
    pick_matrix = (send_slot[None, :] == slot_index[:, None]) & is_live[None, :]
    return pick_matrix, slot_rows, row_place, is_live, dp_count, per_peer, shard_rows


def rebalance(loader_rows, row_counts, row_targets):
    pick_matrix, slot_rows, row_place, is_live, dp_count, per_peer, shard_rows = pick_slots(
        loader_rows, row_counts, row_targets
    )
    slot_count, feature_count = slot_rows.shape
    outgoing = jnp.dot(
        pick_matrix.astype(jnp.bfloat16), slot_rows, preferred_element_type=jnp.float32
    ).astype(jnp.bfloat16)
    out_place = jnp.sum(jnp.where(pick_matrix, row_place[None, :] + 1, 0), axis=1) - 1
    arrived, arrived_place = (
        lax.all_to_all(
            outgoing.reshape(dp_count, per_peer, feature_count),
            "dp",
            split_axis=0,
            concat_axis=0,
            tiled=True,
        ),
        lax.all_to_all(
            out_place.reshape(dp_count, per_peer), "dp", split_axis=0, concat_axis=0, tiled=True
        ),
    )
    land_matrix = (
        arrived_place.reshape(slot_count)[None, :]
        == jnp.arange(shard_rows, dtype=jnp.int32)[:, None]
    ).astype(jnp.bfloat16)
    local_batch = jnp.dot(
        land_matrix, arrived.reshape(slot_count, feature_count), preferred_element_type=jnp.float32
    ).astype(jnp.bfloat16)
    return local_batch


def gathered_plan(loader_rows, row_counts, row_targets, gate_weight, up_weight, down_weight):
    local_batch = rebalance(loader_rows, row_counts, row_targets)
    gate_full, up_full = (
        lax.all_gather(gate_weight, "dp", axis=0, tiled=True),
        lax.all_gather(up_weight, "dp", axis=0, tiled=True),
    )
    travelling = normalize(local_batch)
    hidden = swiglu(lax.all_gather(travelling, "tensor", axis=0, tiled=True), gate_full, up_full)
    summed = lax.psum_scatter(
        rounded_term(hidden, down_weight).astype(jnp.bfloat16),
        "tensor",
        scatter_dimension=0,
        tiled=True,
    ).astype(jnp.float32)
    return (local_batch.astype(jnp.float32) + summed).astype(jnp.bfloat16)


def ff_kernel(
    leaving_ref, leaving_place_ref, gate_ref, up_ref, down_ref, out_ref,
    arrived_v, place_v, batch_v, norm_v, gate_v, up_v, down_v, rows_v, part_out, part_in, hidden_v, term_v, x_in, z_in,
    local_sem, send_sem, recv_sem,
):
    me = lax.axis_index("dp")
    place = lax.axis_index("tensor")
    core, y = lax.rem(me, 2), lax.div(me, 2)
    x, z = lax.rem(place, 2), lax.div(place, 2)
    core_peer = {"dp": 2 * y + 1 - core}
    y_peer = {"dp": 2 * (1 - y) + core}
    corner_peer = {"dp": 2 * (1 - y) + 1 - core}
    x_peer = {"tensor": 2 * z + 1 - x}
    z_peer = {
        1: {"tensor": 2 * (z + 1 - 2 * lax.rem(z, 2)) + x},
        2: {"tensor": 2 * lax.rem(z + 2, 4) + x},
        3: {"tensor": 2 * (3 - z) + x},
    }
    shard_rows, features = batch_v.shape
    half = features // 2
    per_peer = arrived_v.shape[1]
    width = gate_ref.shape[0]
    hidden_width = gate_ref.shape[1]
    tile = 512

    barrier = pltpu.get_barrier_semaphore()
    for peer in (core_peer, y_peer, corner_peer, x_peer, z_peer[1], z_peer[2], z_peer[3]):
        pl.semaphore_signal(barrier, inc=1, device_id=peer, device_id_type=MESH)
    pl.semaphore_wait(barrier, 7)

    sent = []

    def send(src, dst, peer):
        index = len(sent)
        copy = pltpu.make_async_remote_copy(
            src_ref=src,
            dst_ref=dst,
            send_sem=send_sem.at[index],
            recv_sem=recv_sem.at[index],
            device_id=peer,
            device_id_type=MESH,
        )
        copy.start()
        sent.append(copy)
        return copy

    own_cols = pl.ds(pl.multiple_of(y * half, half), half)
    peer_cols = pl.ds(pl.multiple_of((1 - y) * half, half), half)
    own_block = pl.ds(pl.multiple_of(core * width, width), width)
    arrivals = []
    for peer in (y_peer, corner_peer, core_peer):
        block = pl.ds(pl.multiple_of(peer["dp"] * per_peer, per_peer), per_peer)
        arrivals.append(send(leaving_place_ref.at[block, :], place_v.at[me], peer))
        arrivals.append(send(leaving_ref.at[block, :], arrived_v.at[me], peer))
    block = pl.ds(pl.multiple_of(me * per_peer, per_peer), per_peer)
    stay_place = pltpu.make_async_copy(
        leaving_place_ref.at[block, :], place_v.at[me], local_sem.at[4]
    )
    stay_place.start()
    stay = pltpu.make_async_copy(leaving_ref.at[block, :], arrived_v.at[me], local_sem.at[5])
    stay.start()
    gate_swap = send(gate_ref, gate_v.at[own_block, :], core_peer)
    gate_own = pltpu.make_async_copy(gate_ref, gate_v.at[own_block, :], local_sem.at[1])
    gate_own.start()
    up_swap = send(up_ref, up_v.at[own_block, :], core_peer)
    up_own = pltpu.make_async_copy(up_ref, up_v.at[own_block, :], local_sem.at[2])
    up_own.start()
    down_own = pltpu.make_async_copy(down_ref, down_v, local_sem.at[3])
    down_own.start()

    stay_place.wait()
    stay.wait()
    for copy in arrivals:
        copy.wait_recv()
    slots = place_v.shape[0] * per_peer
    places = place_v[...].reshape(slots, place_v.shape[2])
    land = places.astype(jnp.float32).T.astype(jnp.bfloat16)[:shard_rows]
    squares = jnp.zeros((shard_rows, 1), jnp.float32)
    for start in range(0, features, tile):
        cols = slice(start, start + tile)
        wide = jnp.dot(
            land, arrived_v[:, :, cols].reshape(slots, tile), preferred_element_type=jnp.float32
        )
        batch_v[:, cols] = wide.astype(jnp.bfloat16)
        squares = squares + jnp.sum(wide * wide, axis=1, keepdims=True)
    scale = lax.rsqrt(squares / features + 1e-05)
    for start in range(0, features, tile):
        cols = slice(start, start + tile)
        norm_v[:, cols] = (batch_v[:, cols].astype(jnp.float32) * scale).astype(jnp.bfloat16)

    first = send(norm_v.at[:, peer_cols], rows_v.at[0, 0, pl.ds(0, shard_rows), :], y_peer)
    own_rows = pltpu.make_async_copy(
        norm_v.at[:, own_cols], rows_v.at[0, 1, pl.ds(0, shard_rows), :], local_sem.at[0]
    )
    own_rows.start()

    near = pl.ds(0, shard_rows)
    far = pl.ds(shard_rows, shard_rows)
    own_rows.wait()
    first.wait_recv()
    z_copy, x_copy = {}, {}

    def spread(step):
        z_copy[step] = send(
            rows_v.at[0, :, near, :], rows_v.at[step, :, near, :], z_peer[step]
        )

    def cross(step):
        if step:
            z_copy[step].wait_recv()
        x_copy[step] = send(
            rows_v.at[step, :, near, :], rows_v.at[step, :, far, :], x_peer
        )

    parts = {}

    def project(step, compute, pieces):
        for which, weight in ((0, gate_v), (1, up_v)):
            if step == 0 and compute == near:
                (gate_swap, up_swap)[which].wait_recv()
                (gate_own, up_own)[which].wait()

            def body(i, carry):
                cols = pl.ds(pl.multiple_of(i * tile, tile), tile)
                part_out[step, which, compute, cols] = jnp.dot(
                    rows_v[step, 0, compute, :],
                    weight[:, cols],
                    preferred_element_type=jnp.float32,
                ).astype(jnp.bfloat16)
                return carry

            lax.fori_loop(0, hidden_width // tile, body, 0)
            if len(pieces) == 1:
                push(step, which, pieces[0])
        if len(pieces) > 1:
            for piece in pieces:
                push(step, 0, piece)
                push(step, 1, piece)

    def push(step, which, piece):
        parts.setdefault((step, piece.start), []).append(
            send(
                part_out.at[step, which, piece, :], part_in.at[step, which, piece, :], y_peer
            )
        )

    term_copy, pair_copy = {}, {}

    def finish(step, rows_cut, pieces):
        for piece in pieces:
            for copy in parts[step, piece.start]:
                copy.wait_recv()

        def body(i, carry):
            cols = pl.ds(pl.multiple_of(i * tile, tile), tile)
            rows = rows_v[step, 1, rows_cut, :]
            gate_sum = jnp.dot(
                rows, gate_v[:, cols], preferred_element_type=jnp.float32
            ) + part_in[step, 0, rows_cut, cols].astype(jnp.float32)
            up_sum = jnp.dot(
                rows, up_v[:, cols], preferred_element_type=jnp.float32
            ) + part_in[step, 1, rows_cut, cols].astype(jnp.float32)
            hidden_v[rows_cut, cols] = (gate_sum / (1.0 + jnp.exp(-gate_sum)) * up_sum).astype(
                jnp.bfloat16
            )
            return carry

        lax.fori_loop(0, hidden_width // tile, body, 0)
        if step == 0:
            down_own.wait()

        def down_body(i, carry):
            cols = pl.ds(pl.multiple_of(i * tile, tile), tile)
            term_v[step, rows_cut, cols] = jnp.dot(
                hidden_v[rows_cut, :], down_v[:, cols], preferred_element_type=jnp.float32
            ).astype(jnp.bfloat16)
            return carry

        lax.fori_loop(0, 2 * half // tile, down_body, 0)
        if rows_cut != near:
            term_copy[step] = send(term_v.at[step, far, :], x_in.at[step], x_peer)

    def pair(step):
        term_copy[step].wait_recv()
        term_v[step, near, :] = (
            term_v[step, near, :].astype(jnp.float32) + x_in[step].astype(jnp.float32)
        ).astype(jnp.bfloat16)
        pair_copy[step] = send(term_v.at[step, near, :], z_in.at[step - 1], z_peer[step])

    both = pl.ds(0, 2 * shard_rows)
    cross(0)
    spread(2)
    project(0, near, (near,))
    x_copy[0].wait_recv()
    project(0, far, (far,))
    spread(3)
    cross(2)
    project(2, near, (near,))
    x_copy[2].wait_recv()
    project(2, far, (far,))
    spread(1)
    cross(3)
    finish(0, both, (near, far))
    x_copy[3].wait_recv()
    project(3, both, (both,))
    cross(1)
    finish(2, both, (near, far))
    x_copy[1].wait_recv()
    project(1, both, (far, near))
    pair(2)
    finish(3, both, (both,))
    pair(3)
    finish(1, far, (far,))
    finish(1, near, (near,))
    pair(1)
    term_copy[0].wait_recv()
    total = (
        batch_v[...].astype(jnp.float32)
        + term_v[0, near, :].astype(jnp.float32)
        + x_in[0].astype(jnp.float32)
    )
    for step in (2, 3, 1):
        pair_copy[step].wait_recv()
        total = total + z_in[step - 1].astype(jnp.float32)
    out_ref[...] = total.astype(jnp.bfloat16)
    for copy in sent:
        copy.wait_send()


def chip_plan(loader_rows, row_counts, row_targets, gate_weight, up_weight, down_weight):
    pick_matrix, slot_rows, row_place, is_live, dp_count, per_peer, shard_rows = pick_slots(
        loader_rows, row_counts, row_targets
    )
    features = slot_rows.shape[1]
    pick = pick_matrix.astype(jnp.bfloat16)
    lanes = 128
    place_hot = (row_place[:, None] == jnp.arange(lanes, dtype=jnp.int32)[None, :]).astype(
        jnp.bfloat16
    )
    leaving = jnp.dot(pick, slot_rows, preferred_element_type=jnp.float32).astype(jnp.bfloat16)
    leaving_place = jnp.dot(pick, place_hot, preferred_element_type=jnp.float32).astype(
        jnp.bfloat16
    )
    hidden_width = gate_weight.shape[1]
    half = features // 2
    vmem = pl.BlockSpec(memory_space=pltpu.VMEM)
    any_space = pl.BlockSpec(memory_space=pl.ANY)
    bf16 = jnp.bfloat16
    return pl.pallas_call(
        ff_kernel,
        out_shape=jax.ShapeDtypeStruct((shard_rows, features), bf16),
        in_specs=[vmem, vmem, any_space, any_space, any_space],
        out_specs=vmem,
        scratch_shapes=[
            pltpu.VMEM((dp_count, per_peer, features), bf16),
            pltpu.VMEM((dp_count, per_peer, lanes), bf16),
            pltpu.VMEM((shard_rows, features), bf16),
            pltpu.VMEM((shard_rows, features), bf16),
            pltpu.VMEM((half, hidden_width), bf16),
            pltpu.VMEM((half, hidden_width), bf16),
            pltpu.VMEM((hidden_width, features), bf16),
            pltpu.VMEM((4, 2, 2 * shard_rows, half), bf16),
            pltpu.VMEM((4, 2, 2 * shard_rows, hidden_width), bf16),
            pltpu.VMEM((4, 2, 2 * shard_rows, hidden_width), bf16),
            pltpu.VMEM((2 * shard_rows, hidden_width), bf16),
            pltpu.VMEM((4, 2 * shard_rows, features), bf16),
            pltpu.VMEM((4, shard_rows, features), bf16),
            pltpu.VMEM((3, shard_rows, features), bf16),
            pltpu.SemaphoreType.DMA((6,)),
            pltpu.SemaphoreType.DMA((40,)),
            pltpu.SemaphoreType.DMA((40,)),
        ],
        compiler_params=pltpu.CompilerParams(
            collective_id=0, has_side_effects=True, vmem_limit_bytes=62 * 1024 * 1024
        ),
        cost_estimate=pl.CostEstimate(
            flops=26 * 10**9, bytes_accessed=26 * 2**20, transcendentals=2**20
        ),
    )(leaving, leaving_place, gate_weight, up_weight, down_weight)


def per_device(*args):
    if lax.axis_size("dp") == 4 and lax.axis_size("tensor") == 8:
        return chip_plan(*args)
    return gathered_plan(*args)


def solution(mesh):
    placed = (
        P("dp", "tensor", None, None),
        P("dp", "tensor"),
        P("dp", "tensor", None),
        P("dp", "tensor"),
        P("dp", "tensor"),
        P("tensor", None),
    )
    return jax.shard_map(
        per_device, mesh=mesh, in_specs=placed, out_specs=P(("dp", "tensor"), None), check_vma=False
    )
```

```python
import jax
import jax.numpy as jnp
from jax import lax
from jax.experimental import pallas as pl
from jax.experimental.pallas import tpu as pltpu
from jax.sharding import PartitionSpec as P

ROWS_GRP = 512
MESH = pl.DeviceIdType.MESH


def swiglu(inputs, gate_full, up_full):
    gate_act = jnp.dot(inputs, gate_full, preferred_element_type=jnp.float32)
    up_act = jnp.dot(inputs, up_full, preferred_element_type=jnp.float32)
    return (jax.nn.silu(gate_act) * up_act).astype(jnp.bfloat16)


def normalize(row_block):
    wide_rows = row_block.astype(jnp.float32)
    return (
        wide_rows * lax.rsqrt(jnp.mean(wide_rows * wide_rows, axis=1, keepdims=True) + 1e-05)
    ).astype(jnp.bfloat16)


def rounded_term(hidden_part, weights):
    partial_sum = jnp.dot(hidden_part, weights, preferred_element_type=jnp.float32)
    return lax.optimization_barrier(partial_sum.astype(jnp.bfloat16)).astype(jnp.float32)


def pick_slots(loader_rows, row_counts, row_targets):
    dp_count = lax.axis_size("dp")
    tp_count = lax.axis_size("tensor")
    slot_rows = loader_rows[0, 0]
    slot_targets = row_targets[0, 0]
    live_count = row_counts[0, 0]
    slot_count = slot_rows.shape[0]
    feature_count = slot_rows.shape[1]
    per_peer = slot_count // dp_count
    shard_rows = ROWS_GRP // tp_count
    slot_index = jnp.arange(slot_count, dtype=jnp.int32)
    is_live = slot_index < live_count
    peer_index = slot_targets // shard_rows
    row_place = slot_targets % shard_rows
    peer_hot = (
        (peer_index[:, None] == jnp.arange(dp_count, dtype=jnp.int32)[None, :]) & is_live[:, None]
    ).astype(jnp.int32)
    earlier = jnp.cumsum(peer_hot, axis=0) - peer_hot
    slot_rank = jnp.sum(earlier * peer_hot, axis=1)
    send_slot = peer_index * per_peer + slot_rank
    pick_matrix = (send_slot[None, :] == slot_index[:, None]) & is_live[None, :]
    return pick_matrix, slot_rows, row_place, is_live, dp_count, per_peer, shard_rows


def rebalance(loader_rows, row_counts, row_targets):
    pick_matrix, slot_rows, row_place, is_live, dp_count, per_peer, shard_rows = pick_slots(
        loader_rows, row_counts, row_targets
    )
    slot_count, feature_count = slot_rows.shape
    outgoing = jnp.dot(
        pick_matrix.astype(jnp.bfloat16), slot_rows, preferred_element_type=jnp.float32
    ).astype(jnp.bfloat16)
    out_place = jnp.sum(jnp.where(pick_matrix, row_place[None, :] + 1, 0), axis=1) - 1
    arrived, arrived_place = (
        lax.all_to_all(
            outgoing.reshape(dp_count, per_peer, feature_count),
            "dp",
            split_axis=0,
            concat_axis=0,
            tiled=True,
        ),
        lax.all_to_all(
            out_place.reshape(dp_count, per_peer), "dp", split_axis=0, concat_axis=0, tiled=True
        ),
    )
    land_matrix = (
        arrived_place.reshape(slot_count)[None, :]
        == jnp.arange(shard_rows, dtype=jnp.int32)[:, None]
    ).astype(jnp.bfloat16)
    local_batch = jnp.dot(
        land_matrix, arrived.reshape(slot_count, feature_count), preferred_element_type=jnp.float32
    ).astype(jnp.bfloat16)
    return local_batch


def gathered_plan(loader_rows, row_counts, row_targets, gate_weight, up_weight, down_weight):
    local_batch = rebalance(loader_rows, row_counts, row_targets)
    gate_full, up_full = (
        lax.all_gather(gate_weight, "dp", axis=0, tiled=True),
        lax.all_gather(up_weight, "dp", axis=0, tiled=True),
    )
    travelling = normalize(local_batch)
    hidden = swiglu(lax.all_gather(travelling, "tensor", axis=0, tiled=True), gate_full, up_full)
    summed = lax.psum_scatter(
        rounded_term(hidden, down_weight).astype(jnp.bfloat16),
        "tensor",
        scatter_dimension=0,
        tiled=True,
    ).astype(jnp.float32)
    return (local_batch.astype(jnp.float32) + summed).astype(jnp.bfloat16)


def ff_kernel(
    leaving_ref, leaving_place_ref, gate_ref, up_ref, down_ref, out_ref,
    arrived_v, place_v, batch_v, norm_v, gate_v, up_v, down_v, rows_v, part_out, own_v, part_in, hidden_v, term_v, x_in, z_in,
    local_sem, send_sem, recv_sem,
):
    me = lax.axis_index("dp")
    place = lax.axis_index("tensor")
    core, y = lax.rem(me, 2), lax.div(me, 2)
    x, z = lax.rem(place, 2), lax.div(place, 2)
    core_peer = {"dp": 2 * y + 1 - core}
    y_peer = {"dp": 2 * (1 - y) + core}
    corner_peer = {"dp": 2 * (1 - y) + 1 - core}
    x_peer = {"tensor": 2 * z + 1 - x}
    z_peer = {
        1: {"tensor": 2 * (z + 1 - 2 * lax.rem(z, 2)) + x},
        2: {"tensor": 2 * lax.rem(z + 2, 4) + x},
        3: {"tensor": 2 * (3 - z) + x},
    }
    shard_rows, features = batch_v.shape
    half = features // 2
    per_peer = arrived_v.shape[1]
    width = gate_ref.shape[0]
    hidden_width = gate_ref.shape[1]
    tile = 512

    barrier = pltpu.get_barrier_semaphore()
    for peer in (core_peer, y_peer, corner_peer, x_peer, z_peer[1], z_peer[2], z_peer[3]):
        pl.semaphore_signal(barrier, inc=1, device_id=peer, device_id_type=MESH)
    pl.semaphore_wait(barrier, 7)

    sent = []
    counter = list(range(send_sem.shape[0]))

    def send(src, dst, peer):
        index = counter.pop(0)
        copy = pltpu.make_async_remote_copy(
            src_ref=src,
            dst_ref=dst,
            send_sem=send_sem.at[index],
            recv_sem=recv_sem.at[index],
            device_id=peer,
            device_id_type=MESH,
        )
        copy.start()
        sent.append(copy)
        return copy

    own_cols = pl.ds(pl.multiple_of(y * half, half), half)
    peer_cols = pl.ds(pl.multiple_of((1 - y) * half, half), half)
    own_block = pl.ds(pl.multiple_of(core * width, width), width)
    arrivals = []
    for peer in (y_peer, corner_peer, core_peer):
        block = pl.ds(pl.multiple_of(peer["dp"] * per_peer, per_peer), per_peer)
        arrivals.append(send(leaving_place_ref.at[block, :], place_v.at[me], peer))
        arrivals.append(send(leaving_ref.at[block, :], arrived_v.at[me], peer))
    block = pl.ds(pl.multiple_of(me * per_peer, per_peer), per_peer)
    stay_place = pltpu.make_async_copy(
        leaving_place_ref.at[block, :], place_v.at[me], local_sem.at[4]
    )
    stay_place.start()
    stay = pltpu.make_async_copy(leaving_ref.at[block, :], arrived_v.at[me], local_sem.at[5])
    stay.start()
    gate_swap = send(gate_ref, gate_v.at[own_block, :], core_peer)
    gate_own = pltpu.make_async_copy(gate_ref, gate_v.at[own_block, :], local_sem.at[1])
    gate_own.start()
    up_swap = send(up_ref, up_v.at[own_block, :], core_peer)
    up_own = pltpu.make_async_copy(up_ref, up_v.at[own_block, :], local_sem.at[2])
    up_own.start()
    down_own = pltpu.make_async_copy(down_ref, down_v, local_sem.at[3])
    down_own.start()

    stay_place.wait()
    stay.wait()
    for copy in arrivals:
        copy.wait_recv()
    slots = place_v.shape[0] * per_peer
    places = place_v[...].reshape(slots, place_v.shape[2])
    land = places.astype(jnp.float32).T.astype(jnp.bfloat16)[:shard_rows]
    squares = jnp.zeros((shard_rows, 1), jnp.float32)
    for start in range(0, features, tile):
        cols = slice(start, start + tile)
        wide = jnp.dot(
            land, arrived_v[:, :, cols].reshape(slots, tile), preferred_element_type=jnp.float32
        )
        batch_v[:, cols] = wide.astype(jnp.bfloat16)
        squares = squares + jnp.sum(wide * wide, axis=1, keepdims=True)
    scale = lax.rsqrt(squares / features + 1e-05)
    for start in range(0, features, tile):
        cols = slice(start, start + tile)
        norm_v[:, cols] = (batch_v[:, cols].astype(jnp.float32) * scale).astype(jnp.bfloat16)

    first = send(norm_v.at[:, peer_cols], rows_v.at[0, 0, pl.ds(0, shard_rows), :], y_peer)
    own_rows = pltpu.make_async_copy(
        norm_v.at[:, own_cols], rows_v.at[0, 1, pl.ds(0, shard_rows), :], local_sem.at[0]
    )
    own_rows.start()

    near = pl.ds(0, shard_rows)
    far = pl.ds(shard_rows, shard_rows)
    own_rows.wait()
    first.wait_recv()
    z_copy, x_copy = {}, {}

    def spread(step):
        z_copy[step] = send(
            rows_v.at[0, :, near, :], rows_v.at[step, :, near, :], z_peer[step]
        )

    def cross(step):
        if step:
            z_copy[step].wait_recv()
        x_copy[step] = send(
            rows_v.at[step, :, near, :], rows_v.at[step, :, far, :], x_peer
        )

    parts = {}

    slot = {0: 0, 2: 1, 3: 0, 1: 1}
    earlier = {3: 0, 1: 2}

    def project(step, cut, pieces):
        if step in earlier:
            for key in parts:
                if key[0] == earlier[step]:
                    for copy in parts[key]:
                        copy.wait_send()
                        sent[:] = [other for other in sent if other is not copy]
        count = cut.size
        for which, weight in ((0, gate_v), (1, up_v)):
            if step == 0 and cut == near:
                (gate_swap, up_swap)[which].wait_recv()
                (gate_own, up_own)[which].wait()

            def body(i, carry):
                cols = pl.ds(pl.multiple_of(i * tile, tile), tile)
                act = jnp.dot(
                    rows_v[step, :, cut, :].reshape(2 * count, half),
                    weight[:, cols],
                    preferred_element_type=jnp.float32,
                )
                part_out[slot[step], which, cut, cols] = act[:count].astype(jnp.bfloat16)
                own_v[slot[step], which, cut, cols] = act[count:]
                return carry

            lax.fori_loop(0, hidden_width // tile, body, 0)
            if len(pieces) == 1:
                push(step, which, pieces[0])
        if len(pieces) > 1:
            for piece in pieces:
                push(step, 0, piece)
                push(step, 1, piece)

    def push(step, which, piece):
        parts.setdefault((step, piece.start), []).append(
            send(
                part_out.at[slot[step], which, piece, :], part_in.at[step, which, piece, :], y_peer
            )
        )

    term_copy, pair_copy = {}, {}

    def finish(step, rows_cut, pieces):
        for piece in pieces:
            for copy in parts[step, piece.start]:
                copy.wait_recv()

        def body(i, carry):
            cols = pl.ds(pl.multiple_of(i * tile, tile), tile)
            gate_sum = own_v[slot[step], 0, rows_cut, cols] + part_in[
                step, 0, rows_cut, cols
            ].astype(jnp.float32)
            up_sum = own_v[slot[step], 1, rows_cut, cols] + part_in[
                step, 1, rows_cut, cols
            ].astype(jnp.float32)
            hidden_v[rows_cut, cols] = (gate_sum / (1.0 + jnp.exp(-gate_sum)) * up_sum).astype(
                jnp.bfloat16
            )
            return carry

        lax.fori_loop(0, hidden_width // tile, body, 0)
        if step == 0:
            down_own.wait()

        def down_body(i, carry):
            cols = pl.ds(pl.multiple_of(i * tile, tile), tile)
            term_v[step, rows_cut, cols] = jnp.dot(
                hidden_v[rows_cut, :], down_v[:, cols], preferred_element_type=jnp.float32
            ).astype(jnp.bfloat16)
            return carry

        lax.fori_loop(0, 2 * half // tile, down_body, 0)
        if rows_cut != near:
            term_copy[step] = send(term_v.at[step, far, :], x_in.at[step], x_peer)

    def pair(step):
        term_copy[step].wait_recv()
        term_v[step, near, :] = (
            term_v[step, near, :].astype(jnp.float32) + x_in[step].astype(jnp.float32)
        ).astype(jnp.bfloat16)
        pair_copy[step] = send(term_v.at[step, near, :], z_in.at[step - 1], z_peer[step])

    both = pl.ds(0, 2 * shard_rows)
    cross(0)
    spread(2)
    project(0, near, (near,))
    x_copy[0].wait_recv()
    project(0, far, (far,))
    spread(3)
    cross(2)
    x_copy[2].wait_recv()
    project(2, both, (both,))
    spread(1)
    cross(3)
    finish(0, both, (near, far))
    x_copy[3].wait_recv()
    project(3, both, (both,))
    cross(1)
    finish(2, both, (both,))
    x_copy[1].wait_recv()
    project(1, both, (far, near))
    pair(2)
    finish(3, both, (both,))
    pair(3)
    finish(1, far, (far,))
    finish(1, near, (near,))
    pair(1)
    term_copy[0].wait_recv()
    total = (
        batch_v[...].astype(jnp.float32)
        + term_v[0, near, :].astype(jnp.float32)
        + x_in[0].astype(jnp.float32)
    )
    for step in (2, 3, 1):
        pair_copy[step].wait_recv()
        total = total + z_in[step - 1].astype(jnp.float32)
    out_ref[...] = total.astype(jnp.bfloat16)
    for copy in sent:
        copy.wait_send()


def chip_plan(loader_rows, row_counts, row_targets, gate_weight, up_weight, down_weight):
    pick_matrix, slot_rows, row_place, is_live, dp_count, per_peer, shard_rows = pick_slots(
        loader_rows, row_counts, row_targets
    )
    features = slot_rows.shape[1]
    pick = pick_matrix.astype(jnp.bfloat16)
    lanes = 128
    place_hot = (row_place[:, None] == jnp.arange(lanes, dtype=jnp.int32)[None, :]).astype(
        jnp.bfloat16
    )
    leaving = jnp.dot(pick, slot_rows, preferred_element_type=jnp.float32).astype(jnp.bfloat16)
    leaving_place = jnp.dot(pick, place_hot, preferred_element_type=jnp.float32).astype(
        jnp.bfloat16
    )
    hidden_width = gate_weight.shape[1]
    half = features // 2
    vmem = pl.BlockSpec(memory_space=pltpu.VMEM)
    any_space = pl.BlockSpec(memory_space=pl.ANY)
    bf16 = jnp.bfloat16
    return pl.pallas_call(
        ff_kernel,
        out_shape=jax.ShapeDtypeStruct((shard_rows, features), bf16),
        in_specs=[vmem, vmem, any_space, any_space, any_space],
        out_specs=vmem,
        scratch_shapes=[
            pltpu.VMEM((dp_count, per_peer, features), bf16),
            pltpu.VMEM((dp_count, per_peer, lanes), bf16),
            pltpu.VMEM((shard_rows, features), bf16),
            pltpu.VMEM((shard_rows, features), bf16),
            pltpu.VMEM((half, hidden_width), bf16),
            pltpu.VMEM((half, hidden_width), bf16),
            pltpu.VMEM((hidden_width, features), bf16),
            pltpu.VMEM((4, 2, 2 * shard_rows, half), bf16),
            pltpu.VMEM((2, 2, 2 * shard_rows, hidden_width), bf16),
            pltpu.VMEM((2, 2, 2 * shard_rows, hidden_width), jnp.float32),
            pltpu.VMEM((4, 2, 2 * shard_rows, hidden_width), bf16),
            pltpu.VMEM((2 * shard_rows, hidden_width), bf16),
            pltpu.VMEM((4, 2 * shard_rows, features), bf16),
            pltpu.VMEM((4, shard_rows, features), bf16),
            pltpu.VMEM((3, shard_rows, features), bf16),
            pltpu.SemaphoreType.DMA((6,)),
            pltpu.SemaphoreType.DMA((40,)),
            pltpu.SemaphoreType.DMA((40,)),
        ],
        compiler_params=pltpu.CompilerParams(
            collective_id=0, has_side_effects=True, vmem_limit_bytes=62 * 1024 * 1024
        ),
        cost_estimate=pl.CostEstimate(
            flops=26 * 10**9, bytes_accessed=26 * 2**20, transcendentals=2**20
        ),
    )(leaving, leaving_place, gate_weight, up_weight, down_weight)


def per_device(*args):
    if lax.axis_size("dp") == 4 and lax.axis_size("tensor") == 8:
        return chip_plan(*args)
    return gathered_plan(*args)


def solution(mesh):
    placed = (
        P("dp", "tensor", None, None),
        P("dp", "tensor"),
        P("dp", "tensor", None),
        P("dp", "tensor"),
        P("dp", "tensor"),
        P("tensor", None),
    )
    return jax.shard_map(
        per_device, mesh=mesh, in_specs=placed, out_specs=P(("dp", "tensor"), None), check_vma=False
    )
```

```python
import jax
import jax.numpy as jnp
from jax import lax
from jax.experimental import pallas as pl
from jax.experimental.pallas import tpu as pltpu
from jax.sharding import PartitionSpec as P

ROWS_GRP = 512
MESH = pl.DeviceIdType.MESH


def swiglu(inputs, gate_full, up_full):
    gate_act = jnp.dot(inputs, gate_full, preferred_element_type=jnp.float32)
    up_act = jnp.dot(inputs, up_full, preferred_element_type=jnp.float32)
    return (jax.nn.silu(gate_act) * up_act).astype(jnp.bfloat16)


def normalize(row_block):
    wide_rows = row_block.astype(jnp.float32)
    return (
        wide_rows * lax.rsqrt(jnp.mean(wide_rows * wide_rows, axis=1, keepdims=True) + 1e-05)
    ).astype(jnp.bfloat16)


def rounded_term(hidden_part, weights):
    partial_sum = jnp.dot(hidden_part, weights, preferred_element_type=jnp.float32)
    return lax.optimization_barrier(partial_sum.astype(jnp.bfloat16)).astype(jnp.float32)


def pick_slots(loader_rows, row_counts, row_targets):
    dp_count = lax.axis_size("dp")
    tp_count = lax.axis_size("tensor")
    slot_rows = loader_rows[0, 0]
    slot_targets = row_targets[0, 0]
    live_count = row_counts[0, 0]
    slot_count = slot_rows.shape[0]
    feature_count = slot_rows.shape[1]
    per_peer = slot_count // dp_count
    shard_rows = ROWS_GRP // tp_count
    slot_index = jnp.arange(slot_count, dtype=jnp.int32)
    is_live = slot_index < live_count
    peer_index = slot_targets // shard_rows
    row_place = slot_targets % shard_rows
    peer_hot = (
        (peer_index[:, None] == jnp.arange(dp_count, dtype=jnp.int32)[None, :]) & is_live[:, None]
    ).astype(jnp.int32)
    earlier = jnp.cumsum(peer_hot, axis=0) - peer_hot
    slot_rank = jnp.sum(earlier * peer_hot, axis=1)
    send_slot = peer_index * per_peer + slot_rank
    pick_matrix = (send_slot[None, :] == slot_index[:, None]) & is_live[None, :]
    return pick_matrix, slot_rows, row_place, is_live, dp_count, per_peer, shard_rows


def rebalance(loader_rows, row_counts, row_targets):
    pick_matrix, slot_rows, row_place, is_live, dp_count, per_peer, shard_rows = pick_slots(
        loader_rows, row_counts, row_targets
    )
    slot_count, feature_count = slot_rows.shape
    outgoing = jnp.dot(
        pick_matrix.astype(jnp.bfloat16), slot_rows, preferred_element_type=jnp.float32
    ).astype(jnp.bfloat16)
    out_place = jnp.sum(jnp.where(pick_matrix, row_place[None, :] + 1, 0), axis=1) - 1
    arrived, arrived_place = (
        lax.all_to_all(
            outgoing.reshape(dp_count, per_peer, feature_count),
            "dp",
            split_axis=0,
            concat_axis=0,
            tiled=True,
        ),
        lax.all_to_all(
            out_place.reshape(dp_count, per_peer), "dp", split_axis=0, concat_axis=0, tiled=True
        ),
    )
    land_matrix = (
        arrived_place.reshape(slot_count)[None, :]
        == jnp.arange(shard_rows, dtype=jnp.int32)[:, None]
    ).astype(jnp.bfloat16)
    local_batch = jnp.dot(
        land_matrix, arrived.reshape(slot_count, feature_count), preferred_element_type=jnp.float32
    ).astype(jnp.bfloat16)
    return local_batch


def gathered_plan(loader_rows, row_counts, row_targets, gate_weight, up_weight, down_weight):
    local_batch = rebalance(loader_rows, row_counts, row_targets)
    gate_full, up_full = (
        lax.all_gather(gate_weight, "dp", axis=0, tiled=True),
        lax.all_gather(up_weight, "dp", axis=0, tiled=True),
    )
    travelling = normalize(local_batch)
    hidden = swiglu(lax.all_gather(travelling, "tensor", axis=0, tiled=True), gate_full, up_full)
    summed = lax.psum_scatter(
        rounded_term(hidden, down_weight).astype(jnp.bfloat16),
        "tensor",
        scatter_dimension=0,
        tiled=True,
    ).astype(jnp.float32)
    return (local_batch.astype(jnp.float32) + summed).astype(jnp.bfloat16)


def ff_kernel(
    leaving_ref, leaving_place_ref, gate_ref, up_ref, down_ref, out_ref,
    arrived_v, place_v, batch_v, norm_v, gate_v, up_v, down_v, rows_v, part_out, own_v, part_in, hidden_v, term_v, x_in, z_in,
    local_sem, send_sem, recv_sem,
):
    me = lax.axis_index("dp")
    place = lax.axis_index("tensor")
    core, y = lax.rem(me, 2), lax.div(me, 2)
    x, z = lax.rem(place, 2), lax.div(place, 2)
    core_peer = {"dp": 2 * y + 1 - core}
    y_peer = {"dp": 2 * (1 - y) + core}
    corner_peer = {"dp": 2 * (1 - y) + 1 - core}
    x_peer = {"tensor": 2 * z + 1 - x}
    z_peer = {
        1: {"tensor": 2 * (z + 1 - 2 * lax.rem(z, 2)) + x},
        2: {"tensor": 2 * lax.rem(z + 2, 4) + x},
    }
    shard_rows, features = batch_v.shape
    half = features // 2
    per_peer = arrived_v.shape[1]
    width = gate_ref.shape[0]
    hidden_width = gate_ref.shape[1]
    tile = 512

    barrier = pltpu.get_barrier_semaphore()
    for peer in (core_peer, y_peer, corner_peer, x_peer, z_peer[1], z_peer[2]):
        pl.semaphore_signal(barrier, inc=1, device_id=peer, device_id_type=MESH)
    pl.semaphore_wait(barrier, 6)

    sent = []
    counter = list(range(send_sem.shape[0]))

    def send(src, dst, peer):
        index = counter.pop(0)
        copy = pltpu.make_async_remote_copy(
            src_ref=src,
            dst_ref=dst,
            send_sem=send_sem.at[index],
            recv_sem=recv_sem.at[index],
            device_id=peer,
            device_id_type=MESH,
        )
        copy.start()
        sent.append(copy)
        return copy

    own_cols = pl.ds(pl.multiple_of(y * half, half), half)
    peer_cols = pl.ds(pl.multiple_of((1 - y) * half, half), half)
    own_block = pl.ds(pl.multiple_of(core * width, width), width)
    arrivals = []
    for peer in (y_peer, corner_peer, core_peer):
        block = pl.ds(pl.multiple_of(peer["dp"] * per_peer, per_peer), per_peer)
        arrivals.append(send(leaving_place_ref.at[block, :], place_v.at[me], peer))
        arrivals.append(send(leaving_ref.at[block, :], arrived_v.at[me], peer))
    block = pl.ds(pl.multiple_of(me * per_peer, per_peer), per_peer)
    stay_place = pltpu.make_async_copy(
        leaving_place_ref.at[block, :], place_v.at[me], local_sem.at[4]
    )
    stay_place.start()
    stay = pltpu.make_async_copy(leaving_ref.at[block, :], arrived_v.at[me], local_sem.at[5])
    stay.start()
    gate_swap = send(gate_ref, gate_v.at[own_block, :], core_peer)
    gate_own = pltpu.make_async_copy(gate_ref, gate_v.at[own_block, :], local_sem.at[1])
    gate_own.start()
    up_swap = send(up_ref, up_v.at[own_block, :], core_peer)
    up_own = pltpu.make_async_copy(up_ref, up_v.at[own_block, :], local_sem.at[2])
    up_own.start()
    down_own = pltpu.make_async_copy(down_ref, down_v, local_sem.at[3])
    down_own.start()

    stay_place.wait()
    stay.wait()
    for copy in arrivals:
        copy.wait_recv()
    slots = place_v.shape[0] * per_peer
    places = place_v[...].reshape(slots, place_v.shape[2])
    land = places.astype(jnp.float32).T.astype(jnp.bfloat16)[:shard_rows]
    squares = jnp.zeros((shard_rows, 1), jnp.float32)
    for start in range(0, features, tile):
        cols = slice(start, start + tile)
        wide = jnp.dot(
            land, arrived_v[:, :, cols].reshape(slots, tile), preferred_element_type=jnp.float32
        )
        batch_v[:, cols] = wide.astype(jnp.bfloat16)
        squares = squares + jnp.sum(wide * wide, axis=1, keepdims=True)
    scale = lax.rsqrt(squares / features + 1e-05)
    for start in range(0, features, tile):
        cols = slice(start, start + tile)
        norm_v[:, cols] = (batch_v[:, cols].astype(jnp.float32) * scale).astype(jnp.bfloat16)

    first = send(norm_v.at[:, peer_cols], rows_v.at[0, 0, pl.ds(0, shard_rows), :], y_peer)
    own_rows = pltpu.make_async_copy(
        norm_v.at[:, own_cols], rows_v.at[0, 1, pl.ds(0, shard_rows), :], local_sem.at[0]
    )
    own_rows.start()

    near = pl.ds(0, shard_rows)
    far = pl.ds(shard_rows, shard_rows)
    own_rows.wait()
    first.wait_recv()
    z_copy, x_copy = {}, {}

    def spread(step):
        source, peer = (2, z_peer[1]) if step == 3 else (0, z_peer[step])
        z_copy[step] = send(rows_v.at[source, :, near, :], rows_v.at[step, :, near, :], peer)

    def cross(step):
        if step in (1, 3):
            z_copy[step].wait_recv()
        x_copy[step] = send(
            rows_v.at[step, :, near, :], rows_v.at[step, :, far, :], x_peer
        )

    parts = {}

    slot = {0: 0, 1: 1, 3: 0, 2: 1}
    earlier = {3: 0, 2: 1}

    def project(step, cut, pieces):
        if step in earlier:
            for key in parts:
                if key[0] == earlier[step]:
                    for copy in parts[key]:
                        copy.wait_send()
                        sent[:] = [other for other in sent if other is not copy]
        count = cut.size
        for which, weight in ((0, gate_v), (1, up_v)):
            if step == 0 and cut == near:
                (gate_swap, up_swap)[which].wait_recv()
                (gate_own, up_own)[which].wait()

            def body(i, carry):
                cols = pl.ds(pl.multiple_of(i * tile, tile), tile)
                act = jnp.dot(
                    rows_v[step, :, cut, :].reshape(2 * count, half),
                    weight[:, cols],
                    preferred_element_type=jnp.float32,
                )
                part_out[slot[step], which, cut, cols] = act[:count].astype(jnp.bfloat16)
                own_v[slot[step], which, cut, cols] = act[count:]
                return carry

            lax.fori_loop(0, hidden_width // tile, body, 0)
            if len(pieces) == 1:
                push(step, which, pieces[0])
        if len(pieces) > 1:
            for piece in pieces:
                push(step, 0, piece)
                push(step, 1, piece)

    def push(step, which, piece):
        parts.setdefault((step, piece.start), []).append(
            send(
                part_out.at[slot[step], which, piece, :], part_in.at[step, which, piece, :], y_peer
            )
        )

    term_copy, pair_copy = {}, {}

    def finish(step, rows_cut, pieces):
        for piece in pieces:
            for copy in parts[step, piece.start]:
                copy.wait_recv()

        def body(i, carry):
            cols = pl.ds(pl.multiple_of(i * tile, tile), tile)
            gate_sum = own_v[slot[step], 0, rows_cut, cols] + part_in[
                step, 0, rows_cut, cols
            ].astype(jnp.float32)
            up_sum = own_v[slot[step], 1, rows_cut, cols] + part_in[
                step, 1, rows_cut, cols
            ].astype(jnp.float32)
            hidden_v[rows_cut, cols] = (gate_sum / (1.0 + jnp.exp(-gate_sum)) * up_sum).astype(
                jnp.bfloat16
            )
            return carry

        lax.fori_loop(0, hidden_width // tile, body, 0)
        if step == 0:
            down_own.wait()

        def down_body(i, carry):
            cols = pl.ds(pl.multiple_of(i * tile, tile), tile)
            term_v[step, rows_cut, cols] = jnp.dot(
                hidden_v[rows_cut, :], down_v[:, cols], preferred_element_type=jnp.float32
            ).astype(jnp.bfloat16)
            return carry

        lax.fori_loop(0, 2 * half // tile, down_body, 0)
        if rows_cut != near:
            term_copy[step] = send(term_v.at[step, far, :], x_in.at[step], x_peer)

    def pair(step):
        term_copy[step].wait_recv()
        wide = term_v[step, near, :].astype(jnp.float32) + x_in[step].astype(jnp.float32)
        if step == 2:
            pair_copy[3].wait_recv()
            wide = wide + z_in[2].astype(jnp.float32)
        term_v[step, near, :] = wide.astype(jnp.bfloat16)
        pair_copy[step] = send(
            term_v.at[step, near, :], z_in.at[step - 1], z_peer[2 if step == 2 else 1]
        )

    both = pl.ds(0, 2 * shard_rows)
    cross(0)
    spread(1)
    spread(2)
    project(0, near, (near,))
    x_copy[0].wait_recv()
    project(0, far, (far,))
    cross(1)
    project(1, near, (near,))
    z_copy[2].wait_recv()
    spread(3)
    x_copy[1].wait_recv()
    project(1, far, (far,))
    cross(3)
    cross(2)
    finish(0, both, (near, far))
    x_copy[3].wait_recv()
    project(3, both, (both,))
    finish(1, both, (near, far))
    x_copy[2].wait_recv()
    project(2, both, (far, near))
    pair(1)
    finish(3, both, (both,))
    pair(3)
    finish(2, far, (far,))
    finish(2, near, (near,))
    pair(2)
    term_copy[0].wait_recv()
    total = (
        batch_v[...].astype(jnp.float32)
        + term_v[0, near, :].astype(jnp.float32)
        + x_in[0].astype(jnp.float32)
    )
    for step in (1, 2):
        pair_copy[step].wait_recv()
        total = total + z_in[step - 1].astype(jnp.float32)
    out_ref[...] = total.astype(jnp.bfloat16)
    for copy in sent:
        copy.wait_send()


def chip_plan(loader_rows, row_counts, row_targets, gate_weight, up_weight, down_weight):
    pick_matrix, slot_rows, row_place, is_live, dp_count, per_peer, shard_rows = pick_slots(
        loader_rows, row_counts, row_targets
    )
    features = slot_rows.shape[1]
    pick = pick_matrix.astype(jnp.bfloat16)
    lanes = 128
    place_hot = (row_place[:, None] == jnp.arange(lanes, dtype=jnp.int32)[None, :]).astype(
        jnp.bfloat16
    )
    leaving = jnp.dot(pick, slot_rows, preferred_element_type=jnp.float32).astype(jnp.bfloat16)
    leaving_place = jnp.dot(pick, place_hot, preferred_element_type=jnp.float32).astype(
        jnp.bfloat16
    )
    hidden_width = gate_weight.shape[1]
    half = features // 2
    vmem = pl.BlockSpec(memory_space=pltpu.VMEM)
    any_space = pl.BlockSpec(memory_space=pl.ANY)
    bf16 = jnp.bfloat16
    return pl.pallas_call(
        ff_kernel,
        out_shape=jax.ShapeDtypeStruct((shard_rows, features), bf16),
        in_specs=[vmem, vmem, any_space, any_space, any_space],
        out_specs=vmem,
        scratch_shapes=[
            pltpu.VMEM((dp_count, per_peer, features), bf16),
            pltpu.VMEM((dp_count, per_peer, lanes), bf16),
            pltpu.VMEM((shard_rows, features), bf16),
            pltpu.VMEM((shard_rows, features), bf16),
            pltpu.VMEM((half, hidden_width), bf16),
            pltpu.VMEM((half, hidden_width), bf16),
            pltpu.VMEM((hidden_width, features), bf16),
            pltpu.VMEM((4, 2, 2 * shard_rows, half), bf16),
            pltpu.VMEM((2, 2, 2 * shard_rows, hidden_width), bf16),
            pltpu.VMEM((2, 2, 2 * shard_rows, hidden_width), jnp.float32),
            pltpu.VMEM((4, 2, 2 * shard_rows, hidden_width), bf16),
            pltpu.VMEM((2 * shard_rows, hidden_width), bf16),
            pltpu.VMEM((4, 2 * shard_rows, features), bf16),
            pltpu.VMEM((4, shard_rows, features), bf16),
            pltpu.VMEM((3, shard_rows, features), bf16),
            pltpu.SemaphoreType.DMA((6,)),
            pltpu.SemaphoreType.DMA((40,)),
            pltpu.SemaphoreType.DMA((40,)),
        ],
        compiler_params=pltpu.CompilerParams(
            collective_id=0, has_side_effects=True, vmem_limit_bytes=62 * 1024 * 1024
        ),
        cost_estimate=pl.CostEstimate(
            flops=26 * 10**9, bytes_accessed=26 * 2**20, transcendentals=2**20
        ),
    )(leaving, leaving_place, gate_weight, up_weight, down_weight)


def per_device(*args):
    if lax.axis_size("dp") == 4 and lax.axis_size("tensor") == 8:
        return chip_plan(*args)
    return gathered_plan(*args)


def solution(mesh):
    placed = (
        P("dp", "tensor", None, None),
        P("dp", "tensor"),
        P("dp", "tensor", None),
        P("dp", "tensor"),
        P("dp", "tensor"),
        P("tensor", None),
    )
    return jax.shard_map(
        per_device, mesh=mesh, in_specs=placed, out_specs=P(("dp", "tensor"), None), check_vma=False
    )
```

```python
import jax
import jax.numpy as jnp
from jax import lax
from jax.experimental import pallas as pl
from jax.experimental.pallas import tpu as pltpu
from jax.sharding import PartitionSpec as P

ROWS_GRP = 512
MESH = pl.DeviceIdType.MESH


def swiglu(inputs, gate_full, up_full):
    gate_act = jnp.dot(inputs, gate_full, preferred_element_type=jnp.float32)
    up_act = jnp.dot(inputs, up_full, preferred_element_type=jnp.float32)
    return (jax.nn.silu(gate_act) * up_act).astype(jnp.bfloat16)


def normalize(row_block):
    wide_rows = row_block.astype(jnp.float32)
    return (
        wide_rows * lax.rsqrt(jnp.mean(wide_rows * wide_rows, axis=1, keepdims=True) + 1e-05)
    ).astype(jnp.bfloat16)


def rounded_term(hidden_part, weights):
    partial_sum = jnp.dot(hidden_part, weights, preferred_element_type=jnp.float32)
    return lax.optimization_barrier(partial_sum.astype(jnp.bfloat16)).astype(jnp.float32)


def pick_slots(loader_rows, row_counts, row_targets):
    dp_count = lax.axis_size("dp")
    tp_count = lax.axis_size("tensor")
    slot_rows = loader_rows[0, 0]
    slot_targets = row_targets[0, 0]
    live_count = row_counts[0, 0]
    slot_count = slot_rows.shape[0]
    feature_count = slot_rows.shape[1]
    per_peer = slot_count // dp_count
    shard_rows = ROWS_GRP // tp_count
    slot_index = jnp.arange(slot_count, dtype=jnp.int32)
    is_live = slot_index < live_count
    peer_index = slot_targets // shard_rows
    row_place = slot_targets % shard_rows
    peer_hot = (
        (peer_index[:, None] == jnp.arange(dp_count, dtype=jnp.int32)[None, :]) & is_live[:, None]
    ).astype(jnp.int32)
    earlier = jnp.cumsum(peer_hot, axis=0) - peer_hot
    slot_rank = jnp.sum(earlier * peer_hot, axis=1)
    send_slot = peer_index * per_peer + slot_rank
    pick_matrix = (send_slot[None, :] == slot_index[:, None]) & is_live[None, :]
    return pick_matrix, slot_rows, row_place, is_live, dp_count, per_peer, shard_rows


def rebalance(loader_rows, row_counts, row_targets):
    pick_matrix, slot_rows, row_place, is_live, dp_count, per_peer, shard_rows = pick_slots(
        loader_rows, row_counts, row_targets
    )
    slot_count, feature_count = slot_rows.shape
    outgoing = jnp.dot(
        pick_matrix.astype(jnp.bfloat16), slot_rows, preferred_element_type=jnp.float32
    ).astype(jnp.bfloat16)
    out_place = jnp.sum(jnp.where(pick_matrix, row_place[None, :] + 1, 0), axis=1) - 1
    arrived, arrived_place = (
        lax.all_to_all(
            outgoing.reshape(dp_count, per_peer, feature_count),
            "dp",
            split_axis=0,
            concat_axis=0,
            tiled=True,
        ),
        lax.all_to_all(
            out_place.reshape(dp_count, per_peer), "dp", split_axis=0, concat_axis=0, tiled=True
        ),
    )
    land_matrix = (
        arrived_place.reshape(slot_count)[None, :]
        == jnp.arange(shard_rows, dtype=jnp.int32)[:, None]
    ).astype(jnp.bfloat16)
    local_batch = jnp.dot(
        land_matrix, arrived.reshape(slot_count, feature_count), preferred_element_type=jnp.float32
    ).astype(jnp.bfloat16)
    return local_batch


def gathered_plan(loader_rows, row_counts, row_targets, gate_weight, up_weight, down_weight):
    local_batch = rebalance(loader_rows, row_counts, row_targets)
    gate_full, up_full = (
        lax.all_gather(gate_weight, "dp", axis=0, tiled=True),
        lax.all_gather(up_weight, "dp", axis=0, tiled=True),
    )
    travelling = normalize(local_batch)
    hidden = swiglu(lax.all_gather(travelling, "tensor", axis=0, tiled=True), gate_full, up_full)
    summed = lax.psum_scatter(
        rounded_term(hidden, down_weight).astype(jnp.bfloat16),
        "tensor",
        scatter_dimension=0,
        tiled=True,
    ).astype(jnp.float32)
    return (local_batch.astype(jnp.float32) + summed).astype(jnp.bfloat16)


def ff_kernel(
    leaving_ref, leaving_place_ref, gate_ref, up_ref, down_ref, out_ref,
    arrived_v, place_v, batch_v, norm_v, gate_v, up_v, down_v, rows_v, part_out, own_v, part_in, hidden_v, term_v, x_in, z_in,
    local_sem, send_sem, recv_sem,
):
    me = lax.axis_index("dp")
    place = lax.axis_index("tensor")
    core, y = lax.rem(me, 2), lax.div(me, 2)
    x, z = lax.rem(place, 2), lax.div(place, 2)
    core_peer = {"dp": 2 * y + 1 - core}
    y_peer = {"dp": 2 * (1 - y) + core}
    corner_peer = {"dp": 2 * (1 - y) + 1 - core}
    x_peer = {"tensor": 2 * z + 1 - x}
    z_peer = {
        1: {"tensor": 2 * (z + 1 - 2 * lax.rem(z, 2)) + x},
        2: {"tensor": 2 * lax.rem(z + 2, 4) + x},
        3: {"tensor": 2 * (3 - z) + x},
    }
    shard_rows, features = batch_v.shape
    half = features // 2
    per_peer = arrived_v.shape[1]
    width = gate_ref.shape[0]
    hidden_width = gate_ref.shape[1]
    tile = 512

    barrier = pltpu.get_barrier_semaphore()
    for peer in (core_peer, y_peer, corner_peer, x_peer, z_peer[1], z_peer[2], z_peer[3]):
        pl.semaphore_signal(barrier, inc=1, device_id=peer, device_id_type=MESH)
    pl.semaphore_wait(barrier, 7)

    sent = []
    counter = list(range(send_sem.shape[0]))

    def send(src, dst, peer):
        index = counter.pop(0)
        copy = pltpu.make_async_remote_copy(
            src_ref=src,
            dst_ref=dst,
            send_sem=send_sem.at[index],
            recv_sem=recv_sem.at[index],
            device_id=peer,
            device_id_type=MESH,
        )
        copy.start()
        sent.append(copy)
        return copy

    own_cols = pl.ds(pl.multiple_of(y * half, half), half)
    peer_cols = pl.ds(pl.multiple_of((1 - y) * half, half), half)
    own_block = pl.ds(pl.multiple_of(core * width, width), width)
    arrivals = []
    for peer in (y_peer, corner_peer, core_peer):
        block = pl.ds(pl.multiple_of(peer["dp"] * per_peer, per_peer), per_peer)
        arrivals.append(send(leaving_place_ref.at[block, :], place_v.at[me], peer))
        arrivals.append(send(leaving_ref.at[block, :], arrived_v.at[me], peer))
    block = pl.ds(pl.multiple_of(me * per_peer, per_peer), per_peer)
    stay_place = pltpu.make_async_copy(
        leaving_place_ref.at[block, :], place_v.at[me], local_sem.at[4]
    )
    stay_place.start()
    stay = pltpu.make_async_copy(leaving_ref.at[block, :], arrived_v.at[me], local_sem.at[5])
    stay.start()
    gate_swap = send(gate_ref, gate_v.at[own_block, :], core_peer)
    gate_own = pltpu.make_async_copy(gate_ref, gate_v.at[own_block, :], local_sem.at[1])
    gate_own.start()

    stay_place.wait()
    stay.wait()
    for copy in arrivals:
        copy.wait_recv()
    slots = place_v.shape[0] * per_peer
    places = place_v[...].reshape(slots, place_v.shape[2])
    land = places.astype(jnp.float32).T.astype(jnp.bfloat16)[:shard_rows]
    squares = jnp.zeros((shard_rows, 1), jnp.float32)
    for start in range(0, features, tile):
        cols = slice(start, start + tile)
        wide = jnp.dot(
            land, arrived_v[:, :, cols].reshape(slots, tile), preferred_element_type=jnp.float32
        )
        batch_v[:, cols] = wide.astype(jnp.bfloat16)
        squares = squares + jnp.sum(wide * wide, axis=1, keepdims=True)
    scale = lax.rsqrt(squares / features + 1e-05)
    for start in range(0, features, tile):
        cols = slice(start, start + tile)
        norm_v[:, cols] = (batch_v[:, cols].astype(jnp.float32) * scale).astype(jnp.bfloat16)

    first = send(norm_v.at[:, peer_cols], rows_v.at[0, 0, pl.ds(0, shard_rows), :], y_peer)
    own_rows = pltpu.make_async_copy(
        norm_v.at[:, own_cols], rows_v.at[0, 1, pl.ds(0, shard_rows), :], local_sem.at[0]
    )
    own_rows.start()
    up_swap = send(up_ref, up_v.at[own_block, :], core_peer)
    up_own = pltpu.make_async_copy(up_ref, up_v.at[own_block, :], local_sem.at[2])
    up_own.start()
    down_own = pltpu.make_async_copy(down_ref, down_v, local_sem.at[3])
    down_own.start()

    near = pl.ds(0, shard_rows)
    far = pl.ds(shard_rows, shard_rows)
    own_rows.wait()
    first.wait_recv()
    z_copy, x_copy = {}, {}

    def spread(step):
        z_copy[step] = send(
            rows_v.at[0, :, near, :], rows_v.at[step, :, near, :], z_peer[step]
        )

    def cross(step):
        if step:
            z_copy[step].wait_recv()
        x_copy[step] = send(
            rows_v.at[step, :, near, :], rows_v.at[step, :, far, :], x_peer
        )

    parts = {}

    slot = {0: 0, 2: 1, 3: 0, 1: 1}
    earlier = {3: 0, 1: 2}

    def project(step, cut, pieces):
        if step in earlier:
            for key in parts:
                if key[0] == earlier[step]:
                    for copy in parts[key]:
                        copy.wait_send()
                        sent[:] = [other for other in sent if other is not copy]
        count = cut.size
        for which, weight in ((0, gate_v), (1, up_v)):
            if step == 0 and cut == near:
                (gate_swap, up_swap)[which].wait_recv()
                (gate_own, up_own)[which].wait()

            def body(i, carry):
                cols = pl.ds(pl.multiple_of(i * tile, tile), tile)
                act = jnp.dot(
                    rows_v[step, :, cut, :].reshape(2 * count, half),
                    weight[:, cols],
                    preferred_element_type=jnp.float32,
                )
                part_out[slot[step], which, cut, cols] = act[:count].astype(jnp.bfloat16)
                own_v[slot[step], which, cut, cols] = act[count:]
                return carry

            lax.fori_loop(0, hidden_width // tile, body, 0)
            if len(pieces) == 1:
                push(step, which, pieces[0])
        if len(pieces) > 1:
            for piece in pieces:
                push(step, 0, piece)
                push(step, 1, piece)

    def push(step, which, piece):
        parts.setdefault((step, piece.start), []).append(
            send(
                part_out.at[slot[step], which, piece, :], part_in.at[step, which, piece, :], y_peer
            )
        )

    term_copy, pair_copy = {}, {}

    def finish(step, rows_cut, pieces):
        for piece in pieces:
            for copy in parts[step, piece.start]:
                copy.wait_recv()

        def body(i, carry):
            cols = pl.ds(pl.multiple_of(i * tile, tile), tile)
            gate_sum = own_v[slot[step], 0, rows_cut, cols] + part_in[
                step, 0, rows_cut, cols
            ].astype(jnp.float32)
            up_sum = own_v[slot[step], 1, rows_cut, cols] + part_in[
                step, 1, rows_cut, cols
            ].astype(jnp.float32)
            hidden_v[rows_cut, cols] = (gate_sum / (1.0 + jnp.exp(-gate_sum)) * up_sum).astype(
                jnp.bfloat16
            )
            return carry

        lax.fori_loop(0, hidden_width // tile, body, 0)
        if step == 0:
            down_own.wait()

        def down_body(i, carry):
            cols = pl.ds(pl.multiple_of(i * tile, tile), tile)
            term_v[step, rows_cut, cols] = jnp.dot(
                hidden_v[rows_cut, :], down_v[:, cols], preferred_element_type=jnp.float32
            ).astype(jnp.bfloat16)
            return carry

        lax.fori_loop(0, 2 * half // tile, down_body, 0)
        if rows_cut != near:
            term_copy[step] = send(term_v.at[step, far, :], x_in.at[step], x_peer)

    def pair(step):
        term_copy[step].wait_recv()
        term_v[step, near, :] = (
            term_v[step, near, :].astype(jnp.float32) + x_in[step].astype(jnp.float32)
        ).astype(jnp.bfloat16)
        pair_copy[step] = send(term_v.at[step, near, :], z_in.at[step - 1], z_peer[step])

    both = pl.ds(0, 2 * shard_rows)
    cross(0)
    spread(2)
    project(0, near, (near,))
    x_copy[0].wait_recv()
    project(0, far, (far,))
    spread(3)
    cross(2)
    x_copy[2].wait_recv()
    project(2, both, (both,))
    spread(1)
    cross(3)
    finish(0, both, (near, far))
    x_copy[3].wait_recv()
    project(3, both, (both,))
    cross(1)
    finish(2, both, (both,))
    x_copy[1].wait_recv()
    project(1, both, (far, near))
    pair(2)
    finish(3, both, (both,))
    pair(3)
    finish(1, far, (far,))
    finish(1, near, (near,))
    pair(1)
    term_copy[0].wait_recv()
    total = (
        batch_v[...].astype(jnp.float32)
        + term_v[0, near, :].astype(jnp.float32)
        + x_in[0].astype(jnp.float32)
    )
    for step in (2, 3, 1):
        pair_copy[step].wait_recv()
        total = total + z_in[step - 1].astype(jnp.float32)
    out_ref[...] = total.astype(jnp.bfloat16)
    for copy in sent:
        copy.wait_send()


def chip_plan(loader_rows, row_counts, row_targets, gate_weight, up_weight, down_weight):
    pick_matrix, slot_rows, row_place, is_live, dp_count, per_peer, shard_rows = pick_slots(
        loader_rows, row_counts, row_targets
    )
    features = slot_rows.shape[1]
    pick = pick_matrix.astype(jnp.bfloat16)
    lanes = 128
    place_hot = (row_place[:, None] == jnp.arange(lanes, dtype=jnp.int32)[None, :]).astype(
        jnp.bfloat16
    )
    leaving = jnp.dot(pick, slot_rows, preferred_element_type=jnp.float32).astype(jnp.bfloat16)
    leaving_place = jnp.dot(pick, place_hot, preferred_element_type=jnp.float32).astype(
        jnp.bfloat16
    )
    hidden_width = gate_weight.shape[1]
    half = features // 2
    vmem = pl.BlockSpec(memory_space=pltpu.VMEM)
    any_space = pl.BlockSpec(memory_space=pl.ANY)
    bf16 = jnp.bfloat16
    return pl.pallas_call(
        ff_kernel,
        out_shape=jax.ShapeDtypeStruct((shard_rows, features), bf16),
        in_specs=[vmem, vmem, any_space, any_space, any_space],
        out_specs=vmem,
        scratch_shapes=[
            pltpu.VMEM((dp_count, per_peer, features), bf16),
            pltpu.VMEM((dp_count, per_peer, lanes), bf16),
            pltpu.VMEM((shard_rows, features), bf16),
            pltpu.VMEM((shard_rows, features), bf16),
            pltpu.VMEM((half, hidden_width), bf16),
            pltpu.VMEM((half, hidden_width), bf16),
            pltpu.VMEM((hidden_width, features), bf16),
            pltpu.VMEM((4, 2, 2 * shard_rows, half), bf16),
            pltpu.VMEM((2, 2, 2 * shard_rows, hidden_width), bf16),
            pltpu.VMEM((2, 2, 2 * shard_rows, hidden_width), jnp.float32),
            pltpu.VMEM((4, 2, 2 * shard_rows, hidden_width), bf16),
            pltpu.VMEM((2 * shard_rows, hidden_width), bf16),
            pltpu.VMEM((4, 2 * shard_rows, features), bf16),
            pltpu.VMEM((4, shard_rows, features), bf16),
            pltpu.VMEM((3, shard_rows, features), bf16),
            pltpu.SemaphoreType.DMA((6,)),
            pltpu.SemaphoreType.DMA((40,)),
            pltpu.SemaphoreType.DMA((40,)),
        ],
        compiler_params=pltpu.CompilerParams(
            collective_id=0, has_side_effects=True, vmem_limit_bytes=62 * 1024 * 1024
        ),
        cost_estimate=pl.CostEstimate(
            flops=26 * 10**9, bytes_accessed=26 * 2**20, transcendentals=2**20
        ),
    )(leaving, leaving_place, gate_weight, up_weight, down_weight)


def per_device(*args):
    if lax.axis_size("dp") == 4 and lax.axis_size("tensor") == 8:
        return chip_plan(*args)
    return gathered_plan(*args)


def solution(mesh):
    placed = (
        P("dp", "tensor", None, None),
        P("dp", "tensor"),
        P("dp", "tensor", None),
        P("dp", "tensor"),
        P("dp", "tensor"),
        P("tensor", None),
    )
    return jax.shard_map(
        per_device, mesh=mesh, in_specs=placed, out_specs=P(("dp", "tensor"), None), check_vma=False
    )
```
